32 devices in a mesh: rows: 16 (over z, y, x), cols: 2 (over core).
Axes of the slice: x: 2, y: 2, z: 4, core: 2. Of those that a mesh axis runs over, the one named last changes fastest.
Arguments:
- fields: bfloat16 [6144, 512], P('rows', 'cols'), may hold values from -6 to 6
- masks: int32 [6144, 512], P('rows', 'cols'), may hold values from 1 to 256
- offsets: int32 [16, 2], P('rows', 'cols'), may hold values from 0 to 127
Outputs:
- stitched: float32 [4096, 512], P('rows', 'cols')
The draws below stay inside these ranges and needn't reach their ends.
Inputs may be any that keep to these rules, and one draw needn't show every extreme that they name: `offsets`: row offset of a field below its tile's first row.
All inputs are finite; a program needn't handle non-finite values.
Results may differ from the reference program's by a relative error of at most 0.0003.
Values sent between devices are 32-bit elements; how exact they have to be, the bound alone decides.
A program may use at most 64 MiB of HBM per device.

```python
import math
import jax
import jax.numpy as jnp
from jax import lax

ROWS_DEV = 256
COLS_DEV = 256
MARGIN = 128
FIELD_ROWS = 384
NY = 512
N_ROWS = 16
N_COLS = 2


def with_ends(values, rng, low, high):
    dims = values.shape
    index_at = [jax.random.randint(jax.random.fold_in(rng, axis), (), 0, dims[axis]) for axis in range(len(dims))]
    values = values.at[tuple(index_at)].set(low)
    longest = dims.index(max(dims))
    index_at[longest] = (index_at[longest] + 1) % dims[longest]
    return values.at[tuple(index_at)].set(high)


def block_scale(rng, shape, cuts, least, largest):
    def one(axis_at, shards_of):
        heights = jax.random.uniform(jax.random.fold_in(jax.random.fold_in(rng, 6), axis_at), (shards_of,), jnp.float32, least / len(cuts), largest / len(cuts))
        return jnp.repeat(jnp.exp(heights), shape[axis_at] // shards_of).reshape((-1,) + (1,) * (len(shape) - axis_at - 1))

    factor_of = one(*cuts[0])
    for cut in cuts[1:]:
        factor_of = factor_of * one(*cut)
    return factor_of


def scatter_about(own_key, extent, scale, reach, shards=(), kind=jnp.bfloat16):
    drawn = jax.random.normal(own_key, extent, jnp.float32) * scale
    if len(shards) > 0:
        drawn = block_scale(own_key, extent, shards, -0.22, 0.18) * drawn
    return jnp.clip(drawn, min=-reach, max=reach).astype(kind)


def setup_inputs(seed: int = 0) -> dict:
    splits = jax.random.split(jax.random.key(seed), 4)
    return {
        "fields": scatter_about(splits[0], (FIELD_ROWS * N_ROWS, NY), 1.0, 6.0, ((0, 16), (1, 2))),
        "masks": with_ends(jax.random.randint(splits[1], (FIELD_ROWS * N_ROWS, NY), 1, 257), jax.random.fold_in(splits[1], 1), 1, 256).astype(jnp.int32),
        "offsets": with_ends(jax.random.randint(splits[2], (N_ROWS, N_COLS), 0, MARGIN), jax.random.fold_in(splits[2], 1), 0, MARGIN - 1).astype(jnp.int32),
    }


def cosine_forward(values):
    length = values.shape[-1]
    doubled = jnp.concatenate([values, values[..., ::-1]], axis=-1)
    spectrum = jnp.fft.fft(doubled, axis=-1)[..., :length]
    positions = jnp.arange(length)
    rotation = jnp.exp(-1j * (math.pi / (2 * length)) * positions)
    normalizer = jnp.where(positions == 0, math.sqrt(1.0 / length), math.sqrt(2.0 / length))
    return 0.5 * jnp.real(rotation * spectrum) * normalizer

def cosine_inverse(coefficients):
    length = coefficients.shape[-1]
    positions = jnp.arange(length)
    normalizer = jnp.where(positions == 0, math.sqrt(1.0 / length), math.sqrt(2.0 / length))
    rotated = coefficients * normalizer * jnp.exp(1j * (math.pi / (2 * length)) * positions)
    padded = jnp.concatenate([rotated, jnp.zeros_like(rotated)], axis=-1)
    samples = jnp.fft.ifft(padded, axis=-1)[..., :length]
    return jnp.real(samples) * (2.0 * length)

def reference(fields, masks, offsets):
    tile_rows = ROWS_DEV
    tile_cols = COLS_DEV
    field_rows = tile_rows + MARGIN
    strip_rows = tile_rows * N_ROWS
    strip_cols = tile_cols * N_COLS
    picture = fields.astype(jnp.float32).reshape(N_ROWS, field_rows, N_COLS, tile_cols).transpose(0, 2, 1, 3)
    weight = masks.astype(jnp.float32).reshape(N_ROWS, field_rows, N_COLS, tile_cols).transpose(0, 2, 1, 3)
    downward = jnp.concatenate([picture[:, :, 1:] - picture[:, :, :-1], jnp.zeros((N_ROWS, N_COLS, 1, tile_cols), jnp.float32)], axis=2)
    across = jnp.concatenate([picture[..., 1:] - picture[..., :-1], jnp.zeros((N_ROWS, N_COLS, field_rows, 1), jnp.float32)], axis=3)
    stacked = jnp.stack([weight, weight * picture, weight * downward, weight * across], axis=2)

    def placed_canvas(single, begin_at):
        empty = jnp.zeros((4, tile_rows + 2 * MARGIN, tile_cols), jnp.float32)
        return lax.dynamic_update_slice(empty, single, (jnp.int32(0), begin_at.astype(jnp.int32), jnp.int32(0)))
    canvas = jax.vmap(jax.vmap(placed_canvas))(stacked, offsets)
    spillage = canvas[:, :, :, tile_rows:tile_rows + 2 * MARGIN - 1]
    spillage = jnp.concatenate([jnp.zeros_like(spillage[:1]), spillage[:-1]], axis=0)
    totals = canvas[:, :, :, :tile_rows].at[:, :, :, :2 * MARGIN - 1].add(spillage)
    totals = totals.transpose(2, 0, 3, 1, 4).reshape(4, strip_rows, strip_cols)
    divisor = jnp.maximum(totals[0], 1.0)
    composite = totals[1] / divisor
    row_index = jnp.arange(strip_rows)
    col_index = jnp.arange(strip_cols)
    grad_rows = jnp.where((row_index == strip_rows - 1)[:, None], 0.0, totals[2] / divisor)
    grad_cols = totals[3] / divisor
    rows_before = jnp.concatenate([jnp.zeros((1, strip_cols), jnp.float32), grad_rows[:-1]], axis=0)
    cols_before = jnp.concatenate([jnp.zeros((strip_rows, 1), jnp.float32), grad_cols[:, :-1]], axis=1)
    cols_before = jnp.where((col_index % tile_cols == 0)[None, :], 0.0, cols_before)
    divergence = grad_rows - rows_before + (grad_cols - cols_before)
    screen = 16.0 / (tile_cols * tile_cols)
    right_side = screen * composite - divergence
    spectrum = cosine_forward(cosine_forward(right_side).T).T
    row_eigen = 4.0 * jnp.square(jnp.sin(jnp.arange(strip_rows, dtype=jnp.float32) * (math.pi / (2 * strip_rows))))
    col_eigen = 4.0 * jnp.square(jnp.sin(jnp.arange(strip_cols, dtype=jnp.float32) * (math.pi / (2 * strip_cols))))
    denominator = screen + row_eigen[:, None] + col_eigen[None, :]
    quotient = spectrum / denominator
    stitched = cosine_inverse(cosine_inverse(quotient.T).T)
    return stitched
```

```python
import functools
import math

import jax
import jax.numpy as jnp
import numpy as np
from jax import lax
from jax.experimental import pallas as pl
from jax.experimental.pallas import tpu as pltpu
from jax.sharding import PartitionSpec as P

MARGIN = 128
MESH = pl.DeviceIdType.MESH
HIGHEST = lax.Precision.HIGHEST


def cosine_matrix(length):
    k = np.arange(length)[:, None]
    i = np.arange(length)[None, :]
    table = np.cos(np.pi * (((2 * i + 1) * k) % (4 * length)) / (2 * length))
    table *= np.where(k == 0, math.sqrt(1.0 / length), math.sqrt(2.0 / length))
    return table


def make_tables(n, tile_cols, n_rows, n_cols):
    strip_cols = n_cols * tile_cols
    screen = 16.0 / (tile_cols * tile_cols)
    full = cosine_matrix(strip_cols)
    blocks = full.reshape(n_cols, tile_cols, n_cols, tile_cols)
    inverse = blocks.transpose(2, 0, 1, 3)
    forward = blocks.transpose(0, 2, 3, 1)
    local = cosine_matrix(n)
    row_eigen = 4.0 * np.sin(np.pi * np.arange(n) / (2 * n)) ** 2
    col_eigen = 4.0 * np.sin(np.pi * np.arange(strip_cols) / (2 * strip_cols)) ** 2
    mu = screen + col_eigen
    theta = 2.0 * np.arcsinh(np.sqrt(mu) / 2.0)
    edge = np.exp(-theta) / (2.0 * np.sinh(theta))
    q = np.exp(-n * theta)
    params = np.zeros((n_cols, 8, tile_cols))
    params[:, 0] = theta.reshape(n_cols, tile_cols)
    params[:, 1] = (n * theta).reshape(n_cols, tile_cols)
    params[:, 2] = (edge / (1.0 - q ** (2 * n_rows))).reshape(n_cols, tile_cols)
    params[:, 3] = (edge / (1.0 - q * q)).reshape(n_cols, tile_cols)
    params[:, 4] = (edge * q / (1.0 - q * q)).reshape(n_cols, tile_cols)
    params[:, 5] = mu.reshape(n_cols, tile_cols)
    eigen = np.broadcast_to(row_eigen[:, None], (n, 128))
    return [np.ascontiguousarray(t, dtype=np.float32) for t in (forward, inverse, local, local.T, eigen, params)]


def exact(left, right):
    return jnp.dot(left, right, precision=HIGHEST, preferred_element_type=jnp.float32)


def kernel(
    n_rows, n_cols, off_ref, f_ref, m_ref, fwd_hbm, inv_hbm, loc_ref, loct_ref, eig_ref, par_ref,
    out_ref, spill_out, spill_in, xs, ys, mom, fwd, inv, local_t, wave_f, wave_b,
    spill_sem, x_send, x_recv, y_send, y_recv, m_send, m_recv, tab_sem,
):
    a = lax.axis_index("rows")
    b = lax.axis_index("cols")
    n, w = out_ref.shape
    screen = 16.0 / (w * w)

    barrier = pltpu.get_barrier_semaphore()
    for k in range(1, n_rows):
        pl.semaphore_signal(barrier, inc=1, device_id={"rows": lax.rem(a + k, n_rows)}, device_id_type=MESH)
    for k in range(1, n_cols):
        pl.semaphore_signal(barrier, inc=1, device_id={"cols": lax.rem(b + k, n_cols)}, device_id_type=MESH)
    load_fwd = pltpu.make_async_copy(fwd_hbm.at[b], fwd, tab_sem.at[0])
    load_inv = pltpu.make_async_copy(inv_hbm.at[b], inv, tab_sem.at[1])
    load_fwd.start()
    load_inv.start()

    s = off_ref[0, 0]
    height = f_ref.shape[0]
    pair = jnp.concatenate(
        [f_ref[...], m_ref[...].astype(jnp.float32).astype(jnp.bfloat16)], axis=1
    )
    r_at = lax.broadcasted_iota(jnp.int32, (n, height), 0)
    t_at = lax.broadcasted_iota(jnp.int32, (n, height), 1) + s
    one_below = jnp.where(r_at + n == t_at, 1.0, 0.0).astype(jnp.bfloat16)
    one_own = jnp.where(r_at == t_at, 1.0, 0.0).astype(jnp.bfloat16)
    below = jnp.dot(one_below, pair, preferred_element_type=jnp.float32)
    own = jnp.dot(one_own, pair, preferred_element_type=jnp.float32)
    f1 = own[:, :w]
    m1 = own[:, w:]
    row_at = lax.broadcasted_iota(jnp.int32, (n, w), 0)
    col_at = lax.broadcasted_iota(jnp.int32, (n, w), 1)
    last_row = row_at == n - 1
    last_col = col_at == w - 1
    next_f = below[0:1, :w]
    m_end = m1[n - 1 : n]
    g_end = m_end * (next_f - f1[n - 1 : n]) / jnp.maximum(m_end, 1.0)
    spill_out[:, :w] = jnp.where(last_row, g_end, below[:, :w])
    spill_out[:, w:] = below[:, w:]

    pl.semaphore_wait(barrier, n_rows - 1 + n_cols - 1)
    spill_copy = pltpu.make_async_remote_copy(
        src_ref=spill_out, dst_ref=spill_in, send_sem=spill_sem.at[0], recv_sem=spill_sem.at[1],
        device_id={"rows": lax.rem(a + 1, n_rows)}, device_id_type=MESH,
    )

    @pl.when(a < n_rows - 1)
    def _():
        spill_copy.start()

    f1_next = jnp.where(last_row, next_f, pltpu.roll(f1, n - 1, 0))
    p1 = m1 * f1
    sx1 = m1 * (f1_next - f1)
    sy1 = m1 * jnp.where(last_col, 0.0, pltpu.roll(f1, w - 1, 1) - f1)
    theta = par_ref[b, 0:1]
    n_theta = par_ref[b, 1:2]
    wide_edge = par_ref[b, 2:3]
    tile_edge = par_ref[b, 3:4]
    tile_edge_q = par_ref[b, 4:5]
    mu = par_ref[b, 5:6]
    row_f = row_at.astype(jnp.float32)
    wave_b[...] = jnp.exp(-theta * row_f)
    wave_f[...] = jnp.exp(-theta * ((n - 1) - row_f))

    @pl.when(a == 0)
    def _():
        spill_in[...] = jnp.zeros_like(spill_in)

    @pl.when(a > 0)
    def _():
        spill_copy.wait_recv()

    f2 = spill_in[:, :w]
    m2 = spill_in[:, w:]
    m2_next = pltpu.roll(m2, n - 1, 0)
    down2 = jnp.where(m2_next > 0.0, pltpu.roll(f2, n - 1, 0) - f2, 0.0)
    across2 = jnp.where(last_col, 0.0, pltpu.roll(f2, w - 1, 1) - f2)
    scale = 1.0 / jnp.maximum(m1 + m2, 1.0)
    composite = (p1 + m2 * f2) * scale
    gx = (sx1 + m2 * down2) * scale
    gx = jnp.where(last_row & (a == n_rows - 1), 0.0, gx)
    gy = (sy1 + m2 * across2) * scale
    gx_before = jnp.where(row_at == 0, spill_in[n - 1 : n, :w], pltpu.roll(gx, 1, 0))
    gy_before = jnp.where(col_at == 0, 0.0, pltpu.roll(gy, 1, 1))
    xs[b] = screen * composite - ((gx - gx_before) + (gy - gy_before))

    def swap(buf, send, recv):
        copies = []
        for k in range(1, n_cols):
            to = lax.rem(b + k, n_cols)
            copies.append(
                pltpu.make_async_remote_copy(
                    src_ref=buf.at[b], dst_ref=buf.at[b], send_sem=send.at[k], recv_sem=recv.at[k],
                    device_id={"cols": to}, device_id_type=MESH,
                )
            )
            copies[-1].start()
        return copies

    def gathered(buf, copies, table):
        total = exact(buf[b], table[b])
        for k in range(1, n_cols):
            copies[k - 1].wait_recv()
            at = lax.rem(b + n_cols - k, n_cols)
            total += exact(buf[at], table[at])
        return total

    x_copies = swap(xs, x_send, x_recv)
    load_fwd.wait()
    spectral = gathered(xs, x_copies, fwd)

    mom_f = jnp.sum(wave_f[...] * spectral, axis=0, keepdims=True)
    mom_b = jnp.sum(wave_b[...] * spectral, axis=0, keepdims=True)
    sub = lax.broadcasted_iota(jnp.int32, (8, w), 0)
    mom[a] = jnp.where(sub == 0, mom_f, jnp.where(sub == 1, mom_b, 0.0))
    m_copies = []
    for k in range(1, n_rows):
        m_copies.append(
            pltpu.make_async_remote_copy(
                src_ref=mom.at[a], dst_ref=mom.at[a], send_sem=m_send.at[k], recv_sem=m_recv.at[k],
                device_id={"rows": lax.rem(a + k, n_rows)}, device_id_type=MESH,
            )
        )
        m_copies[-1].start()
    eig = jnp.concatenate([eig_ref[...]] * (w // 128), axis=1)
    quotient = exact(loc_ref[...], spectral) / (eig + mu)
    local_t[...] = exact(loct_ref[...], quotient)
    for copy in m_copies:
        copy.wait_recv()
    period = 2 * n_rows
    top = jnp.zeros((8, w), jnp.float32)
    bottom = jnp.zeros((8, w), jnp.float32)
    for other in range(n_rows):
        e_top = jnp.where(sub == 0, lax.rem(a - 1 - other + period, period), a + other)
        e_bottom = jnp.where(sub == 0, period - 2 - a - other, lax.rem(other - a - 1 + period, period))
        held = mom[other]
        top += jnp.exp(-n_theta * e_top.astype(jnp.float32)) * held
        bottom += jnp.exp(-n_theta * e_bottom.astype(jnp.float32)) * held
    from_top = wide_edge * jnp.sum(top, axis=0, keepdims=True) - (tile_edge * mom_b + tile_edge_q * mom_f)
    from_bottom = wide_edge * jnp.sum(bottom, axis=0, keepdims=True) - (tile_edge * mom_f + tile_edge_q * mom_b)
    ys[b] = local_t[...] + wave_b[...] * from_top + wave_f[...] * from_bottom

    y_copies = swap(ys, y_send, y_recv)
    load_inv.wait()
    out_ref[...] = gathered(ys, y_copies, inv)

    for copy in x_copies + y_copies + m_copies:
        copy.wait_send()

    @pl.when(a < n_rows - 1)
    def _():
        spill_copy.wait_send()


def shards(n_rows, n_cols, fields, masks, offsets):
    n = fields.shape[0] - MARGIN
    w = fields.shape[1]
    tables = make_tables(n, w, n_rows, n_cols)
    vmem = pl.BlockSpec(memory_space=pltpu.VMEM)
    anywhere = pl.BlockSpec(memory_space=pl.ANY)
    f32 = jnp.float32
    return pl.pallas_call(
        functools.partial(kernel, n_rows, n_cols),
        out_shape=jax.ShapeDtypeStruct((n, w), f32),
        in_specs=[pl.BlockSpec(memory_space=pltpu.SMEM), vmem, vmem, anywhere, anywhere] + [vmem] * 4,
        out_specs=vmem,
        scratch_shapes=[
            pltpu.VMEM((n, 2 * w), f32),
            pltpu.VMEM((n, 2 * w), f32),
            pltpu.VMEM((n_cols, n, w), f32),
            pltpu.VMEM((n_cols, n, w), f32),
            pltpu.VMEM((n_rows, 8, w), f32),
            pltpu.VMEM((n_cols, w, w), f32),
            pltpu.VMEM((n_cols, w, w), f32),
            pltpu.VMEM((n, w), f32),
            pltpu.VMEM((n, w), f32),
            pltpu.VMEM((n, w), f32),
            pltpu.SemaphoreType.DMA((2,)),
            pltpu.SemaphoreType.DMA((n_cols,)),
            pltpu.SemaphoreType.DMA((n_cols,)),
            pltpu.SemaphoreType.DMA((n_cols,)),
            pltpu.SemaphoreType.DMA((n_cols,)),
            pltpu.SemaphoreType.DMA((n_rows,)),
            pltpu.SemaphoreType.DMA((n_rows,)),
            pltpu.SemaphoreType.DMA((2,)),
        ],
        compiler_params=pltpu.CompilerParams(
            collective_id=0, has_side_effects=True, vmem_limit_bytes=56 * 1024 * 1024
        ),
    )(offsets, fields, masks, *tables)


def solution(mesh):
    placed = (P("rows", "cols"), P("rows", "cols"), P("rows", "cols"))
    body = functools.partial(shards, mesh.shape["rows"], mesh.shape["cols"])
    return jax.shard_map(body, mesh=mesh, in_specs=placed, out_specs=P("rows", "cols"), check_vma=False)
```

```python
import functools
import math

import jax
import jax.numpy as jnp
import numpy as np
from jax import lax
from jax.experimental import pallas as pl
from jax.experimental.pallas import tpu as pltpu
from jax.sharding import PartitionSpec as P

MARGIN = 128
MESH = pl.DeviceIdType.MESH
HIGHEST = lax.Precision.HIGHEST


def cosine_matrix(length):
    k = np.arange(length)[:, None]
    i = np.arange(length)[None, :]
    table = np.cos(np.pi * (((2 * i + 1) * k) % (4 * length)) / (2 * length))
    table *= np.where(k == 0, math.sqrt(1.0 / length), math.sqrt(2.0 / length))
    return table


def make_tables(n, tile_cols, n_rows, n_cols):
    strip_cols = n_cols * tile_cols
    screen = 16.0 / (tile_cols * tile_cols)
    full = cosine_matrix(strip_cols)
    blocks = full.reshape(n_cols, tile_cols, n_cols, tile_cols)
    inverse = blocks.transpose(2, 0, 1, 3)
    forward = blocks.transpose(0, 2, 3, 1)
    local = cosine_matrix(n)
    row_eigen = 4.0 * np.sin(np.pi * np.arange(n) / (2 * n)) ** 2
    col_eigen = 4.0 * np.sin(np.pi * np.arange(strip_cols) / (2 * strip_cols)) ** 2
    mu = screen + col_eigen
    theta = 2.0 * np.arcsinh(np.sqrt(mu) / 2.0)
    edge = np.exp(-theta) / (2.0 * np.sinh(theta))
    q = np.exp(-n * theta)
    params = np.zeros((n_cols, 8, tile_cols))
    params[:, 0] = theta.reshape(n_cols, tile_cols)
    params[:, 1] = (n * theta).reshape(n_cols, tile_cols)
    params[:, 2] = (edge / (1.0 - q ** (2 * n_rows))).reshape(n_cols, tile_cols)
    params[:, 3] = (edge / (1.0 - q * q)).reshape(n_cols, tile_cols)
    params[:, 4] = (edge * q / (1.0 - q * q)).reshape(n_cols, tile_cols)
    params[:, 5] = mu.reshape(n_cols, tile_cols)
    eigen = np.broadcast_to(row_eigen[:, None], (n, 128))
    both = np.stack([local, local.T])
    return [np.ascontiguousarray(t, dtype=np.float32) for t in (forward, inverse, both, eigen, params)]


CHUNKS = 4
LAG = 8


def exact(left, right):
    return jnp.dot(left, right, precision=HIGHEST, preferred_element_type=jnp.float32)


def kernel(
    n_rows, n_cols, off_ref, f_hbm, m_hbm, fwd_hbm, inv_hbm, loc_hbm, eig_hbm, par_hbm,
    out_ref, f_ref, m_ref, fwd, inv, loc, eig_ref, par_ref,
    spill_out, spill_in, own, xs, spec, ys, mom, weigh, coef, wave_f, wave_b,
    tab_sem, spill_send, spill_recv, x_send, x_recv, y_send, y_recv, m_send, m_recv, c_send, c_recv,
):
    a = lax.axis_index("rows")
    b = lax.axis_index("cols")
    n, w = out_ref.shape
    step = n // CHUNKS
    screen = 16.0 / (w * w)
    f32 = jnp.float32

    def load(k, src, dst):
        copy = pltpu.make_async_copy(src, dst, tab_sem.at[k])
        copy.start()
        return copy

    load_m = load(0, m_hbm, m_ref)
    load_f = load(1, f_hbm, f_ref)
    barrier = pltpu.get_barrier_semaphore()
    for k in range(1, n_rows):
        pl.semaphore_signal(barrier, inc=1, device_id={"rows": lax.rem(a + k, n_rows)}, device_id_type=MESH)
    for k in range(1, n_cols):
        pl.semaphore_signal(barrier, inc=1, device_id={"cols": lax.rem(b + k, n_cols)}, device_id_type=MESH)
    load_par = load(2, par_hbm, par_ref)
    load_fwd = load(3, fwd_hbm.at[b], fwd)
    load_loc = load(4, loc_hbm, loc)
    load_eig = load(5, eig_hbm, eig_ref)
    load_inv = load(6, inv_hbm.at[b], inv)

    s = off_ref[0, 0]

    def placing(first_row, count, first_t):
        r_at = lax.broadcasted_iota(jnp.int32, (count, n), 0) + first_row
        t_at = lax.broadcasted_iota(jnp.int32, (count, n), 1) + (first_t + s)
        return jnp.where(r_at == t_at, 1.0, 0.0).astype(jnp.bfloat16)

    def placed(matrix, pair):
        return jnp.dot(matrix, pair, preferred_element_type=f32)

    def pair_of(start):
        rows = pl.ds(start, n)
        return jnp.concatenate(
            [f_ref[rows, :], m_ref[rows, :].astype(f32).astype(jnp.bfloat16)], axis=1
        )

    first = placing(n - 2 * LAG, step + 2 * LAG, MARGIN)
    load_m.wait()
    load_f.wait()
    pair_low = pair_of(MARGIN)
    block = placed(first, pair_low)
    end_f, end_m = block[2 * LAG - 1 : 2 * LAG, :w], block[2 * LAG - 1 : 2 * LAG, w:]
    g_end = end_m * (block[2 * LAG : 2 * LAG + 1, :w] - end_f) / jnp.maximum(end_m, 1.0)
    spill_out[:LAG, :w] = jnp.broadcast_to(g_end, (LAG, w))
    spill_out[:LAG, w:] = jnp.zeros((LAG, w), f32)
    spill_out[LAG : LAG + step, :] = block[2 * LAG :]
    own[n : n + LAG, :] = block[2 * LAG : 3 * LAG]

    pl.semaphore_wait(barrier, n_rows - 1 + n_cols - 1)
    spill_copies = []
    for c in range(CHUNKS):
        lo = 0 if c == 0 else LAG + c * step
        rows = pl.ds(lo, LAG + (c + 1) * step - lo)
        if c > 0:
            spill_out[rows, :] = placed(placing(n + c * step, step, MARGIN), pair_low)
        spill_copies.append(
            pltpu.make_async_remote_copy(
                src_ref=spill_out.at[rows], dst_ref=spill_in.at[rows],
                send_sem=spill_send.at[c], recv_sem=spill_recv.at[c],
                device_id={"rows": lax.rem(a + 1, n_rows)}, device_id_type=MESH,
            )
        )
        pl.when(a < n_rows - 1)(spill_copies[-1].start)

    own[:n, :] = placed(placing(0, n, 0), pair_of(0))
    load_par.wait()
    row_f = lax.broadcasted_iota(jnp.int32, (n, w), 0).astype(f32)
    for c in range(n_cols):
        theta = par_ref[c, 0:1]
        wave_b[c] = jnp.exp(-theta * row_f)
        wave_f[c] = jnp.exp(-theta * ((n - 1) - row_f))
    n_theta = par_ref[b, 1:2]
    wide_edge = par_ref[b, 2:3]
    tile_edge = par_ref[b, 3:4]
    tile_edge_q = par_ref[b, 4:5]
    mu = par_ref[b, 5:6]
    period = 2 * n_rows

    def weight(power):
        return wide_edge * jnp.exp(-n_theta * power.astype(f32))

    for other in range(n_rows):
        weigh[0, other] = jnp.concatenate(
            [weight(lax.rem(a - 1 - other + period, period)), weight(a + other)], axis=1
        )
        weigh[1, other] = jnp.concatenate(
            [weight(period - 2 - a - other), weight(lax.rem(other - a - 1 + period, period))], axis=1
        )
    load_fwd.wait()
    spill_in[LAG + n :, :] = jnp.zeros((LAG, 2 * w), f32)

    @pl.when(a == 0)
    def _():
        spill_in[: LAG + n, :] = jnp.zeros((LAG + n, 2 * w), f32)

    def swap(buf, rows, send, recv, c):
        copies = []
        for k in range(1, n_cols):
            copies.append(
                pltpu.make_async_remote_copy(
                    src_ref=buf.at[b, rows], dst_ref=buf.at[b, rows],
                    send_sem=send.at[k, c], recv_sem=recv.at[k, c],
                    device_id={"cols": lax.rem(b + k, n_cols)}, device_id_type=MESH,
                )
            )
            copies[-1].start()
        return copies

    bounds = [0] + [c * step - LAG for c in range(1, CHUNKS)] + [n]
    mom_f = jnp.zeros((1, w), f32)
    mom_b = jnp.zeros((1, w), f32)
    gx_last = None
    swaps = []

    def transform(c, mom_f, mom_b):
        lo, hi = bounds[c], bounds[c + 1]
        total = exact(xs[b, lo:hi], fwd[b])
        for k in range(1, n_cols):
            swaps[c][k - 1].wait_recv()
            at = lax.rem(b + n_cols - k, n_cols)
            total += exact(xs[at, lo:hi], fwd[at])
        spec[lo:hi, :] = total
        mom_f += jnp.sum(wave_f[b, lo:hi] * total, axis=0, keepdims=True)
        mom_b += jnp.sum(wave_b[b, lo:hi] * total, axis=0, keepdims=True)
        return mom_f, mom_b

    for c in range(CHUNKS):
        lo, hi = bounds[c], bounds[c + 1]
        count = hi - lo
        pl.when(a > 0)(spill_copies[c].wait_recv)
        row_at = lax.broadcasted_iota(jnp.int32, (count, w), 0)
        col_at = lax.broadcasted_iota(jnp.int32, (count, w), 1)
        last_col = col_at == w - 1
        f1, m1 = own[lo:hi, :w], own[lo:hi, w:]
        f2, m2 = spill_in[LAG + lo : LAG + hi, :w], spill_in[LAG + lo : LAG + hi, w:]
        down1 = own[lo + 1 : hi + 1, :w] - f1
        under = spill_in[LAG + lo + 1 : LAG + hi + 1, :]
        down2 = jnp.where(under[:, w:] > 0.0, under[:, :w] - f2, 0.0)
        across1 = jnp.where(last_col, 0.0, pltpu.roll(f1, w - 1, 1) - f1)
        across2 = jnp.where(last_col, 0.0, pltpu.roll(f2, w - 1, 1) - f2)
        scale = 1.0 / jnp.maximum(m1 + m2, 1.0)
        composite = (m1 * f1 + m2 * f2) * scale
        gx = (m1 * down1 + m2 * down2) * scale
        if c == CHUNKS - 1:
            gx = jnp.where((row_at == count - 1) & (a == n_rows - 1), 0.0, gx)
        gy = (m1 * across1 + m2 * across2) * scale
        before = spill_in[LAG - 1 : LAG, :w] if c == 0 else gx_last
        gx_before = jnp.where(row_at == 0, before, pltpu.roll(gx, 1, 0))
        gy_before = jnp.where(col_at == 0, 0.0, pltpu.roll(gy, 1, 1))
        gx_last = gx[count - 1 : count]
        xs[b, lo:hi] = screen * composite - ((gx - gx_before) + (gy - gy_before))
        swaps.append(swap(xs, pl.ds(lo, count), x_send, x_recv, c))
        if c > 0:
            mom_f, mom_b = transform(c - 1, mom_f, mom_b)
    mom_f, mom_b = transform(CHUNKS - 1, mom_f, mom_b)

    mom[a] = jnp.concatenate([mom_f, mom_b], axis=1)
    m_copies = []
    for k in range(1, n_rows):
        m_copies.append(
            pltpu.make_async_remote_copy(
                src_ref=mom.at[a], dst_ref=mom.at[a], send_sem=m_send.at[k], recv_sem=m_recv.at[k],
                device_id={"rows": lax.rem(a + k, n_rows)}, device_id_type=MESH,
            )
        )
        m_copies[-1].start()
    load_loc.wait()
    load_eig.wait()
    eig = jnp.concatenate([eig_ref[...]] * (w // 128), axis=1)
    quotient = exact(loc[0], spec[...]) / (eig + mu)
    ys[b] = exact(loc[1], quotient)
    swaps.append(swap(ys, pl.ds(0, n), y_send, y_recv, 0))
    load_inv.wait()
    for copy in m_copies:
        copy.wait_recv()
    top = jnp.zeros((1, 2 * w), f32)
    bottom = jnp.zeros((1, 2 * w), f32)
    for other in range(n_rows):
        top += weigh[0, other] * mom[other]
        bottom += weigh[1, other] * mom[other]
    from_top = top[:, :w] + top[:, w:] - (tile_edge * mom_b + tile_edge_q * mom_f)
    from_bottom = bottom[:, :w] + bottom[:, w:] - (tile_edge * mom_f + tile_edge_q * mom_b)
    coef[b] = jnp.concatenate([from_top, from_bottom], axis=1)
    swaps.append(swap(coef, pl.ds(0, 1), c_send, c_recv, 0))

    def part(at):
        pair = coef[at]
        return exact(ys[at] + wave_b[at] * pair[:, :w] + wave_f[at] * pair[:, w:], inv[at])

    total = part(b)
    for k in range(1, n_cols):
        swaps[-2][k - 1].wait_recv()
        swaps[-1][k - 1].wait_recv()
        total += part(lax.rem(b + n_cols - k, n_cols))
    out_ref[...] = total

    for copies in swaps + [m_copies]:
        for copy in copies:
            copy.wait_send()
    for copy in spill_copies:
        pl.when(a < n_rows - 1)(copy.wait_send)


def shards(n_rows, n_cols, fields, masks, offsets):
    height, w = fields.shape
    n = height - MARGIN
    tables = make_tables(n, w, n_rows, n_cols)
    vmem = pl.BlockSpec(memory_space=pltpu.VMEM)
    anywhere = pl.BlockSpec(memory_space=pl.ANY)
    f32 = jnp.float32
    dma = pltpu.SemaphoreType.DMA
    return pl.pallas_call(
        functools.partial(kernel, n_rows, n_cols),
        out_shape=jax.ShapeDtypeStruct((n, w), f32),
        in_specs=[pl.BlockSpec(memory_space=pltpu.SMEM)] + [anywhere] * 7,
        out_specs=vmem,
        scratch_shapes=[
            pltpu.VMEM((height, w), fields.dtype),
            pltpu.VMEM((height, w), masks.dtype),
            pltpu.VMEM((n_cols, w, w), f32),
            pltpu.VMEM((n_cols, w, w), f32),
            pltpu.VMEM((2, n, n), f32),
            pltpu.VMEM((n, 128), f32),
            pltpu.VMEM((n_cols, 8, w), f32),
            pltpu.VMEM((n + LAG, 2 * w), f32),
            pltpu.VMEM((n + 2 * LAG, 2 * w), f32),
            pltpu.VMEM((n + LAG, 2 * w), f32),
            pltpu.VMEM((n_cols, n, w), f32),
            pltpu.VMEM((n, w), f32),
            pltpu.VMEM((n_cols, n, w), f32),
            pltpu.VMEM((n_rows, 1, 2 * w), f32),
            pltpu.VMEM((2, n_rows, 1, 2 * w), f32),
            pltpu.VMEM((n_cols, 1, 2 * w), f32),
            pltpu.VMEM((n_cols, n, w), f32),
            pltpu.VMEM((n_cols, n, w), f32),
            dma((7,)),
            dma((CHUNKS,)),
            dma((CHUNKS,)),
            dma((n_cols, CHUNKS)),
            dma((n_cols, CHUNKS)),
            dma((n_cols, 1)),
            dma((n_cols, 1)),
            dma((n_rows,)),
            dma((n_rows,)),
            dma((n_cols, 1)),
            dma((n_cols, 1)),
        ],
        compiler_params=pltpu.CompilerParams(
            collective_id=0, has_side_effects=True, vmem_limit_bytes=56 * 1024 * 1024
        ),
    )(offsets, fields, masks, *tables)


def solution(mesh):
    placed = (P("rows", "cols"), P("rows", "cols"), P("rows", "cols"))
    body = functools.partial(shards, mesh.shape["rows"], mesh.shape["cols"])
    return jax.shard_map(body, mesh=mesh, in_specs=placed, out_specs=P("rows", "cols"), check_vma=False)
```

```python
import functools
import math

import jax
import jax.numpy as jnp
import numpy as np
from jax import lax
from jax.experimental import pallas as pl
from jax.experimental.pallas import tpu as pltpu
from jax.sharding import PartitionSpec as P

MARGIN = 128
MESH = pl.DeviceIdType.MESH
HIGHEST = lax.Precision.HIGHEST


def cosine_matrix(length):
    k = np.arange(length)[:, None]
    i = np.arange(length)[None, :]
    table = np.cos(np.pi * (((2 * i + 1) * k) % (4 * length)) / (2 * length))
    table *= np.where(k == 0, math.sqrt(1.0 / length), math.sqrt(2.0 / length))
    return table


def make_tables(n, tile_cols, n_rows, n_cols):
    strip_cols = n_cols * tile_cols
    screen = 16.0 / (tile_cols * tile_cols)
    full = cosine_matrix(strip_cols)
    blocks = full.reshape(n_cols, tile_cols, n_cols, tile_cols)
    inverse = blocks.transpose(2, 0, 1, 3)
    forward = blocks.transpose(2, 0, 3, 1)
    inverse = inverse.astype(np.float32)
    high = inverse.astype(jnp.bfloat16)
    low = (inverse - high.astype(np.float32)).astype(jnp.bfloat16)
    inverse = np.stack([high, low], axis=2)
    local = cosine_matrix(n)
    row_eigen = 4.0 * np.sin(np.pi * np.arange(n) / (2 * n)) ** 2
    col_eigen = 4.0 * np.sin(np.pi * np.arange(strip_cols) / (2 * strip_cols)) ** 2
    mu = screen + col_eigen
    theta = 2.0 * np.arcsinh(np.sqrt(mu) / 2.0)
    edge = np.exp(-theta) / (2.0 * np.sinh(theta))
    q = np.exp(-n * theta)
    params = np.zeros((n_cols, 8, tile_cols))
    params[:, 0] = theta.reshape(n_cols, tile_cols)
    params[:, 1] = (n * theta).reshape(n_cols, tile_cols)
    params[:, 2] = (edge / (1.0 - q ** (2 * n_rows))).reshape(n_cols, tile_cols)
    params[:, 3] = (edge / (1.0 - q * q)).reshape(n_cols, tile_cols)
    params[:, 4] = (edge * q / (1.0 - q * q)).reshape(n_cols, tile_cols)
    params[:, 5] = mu.reshape(n_cols, tile_cols)
    eigen = np.broadcast_to(row_eigen[:, None], (n, 128))
    both = np.stack([local, local.T])
    forward, both, eigen, params = [
        np.ascontiguousarray(t, dtype=np.float32) for t in (forward, both, eigen, params)
    ]
    return forward, inverse, both, eigen, params


CHUNKS = 4
LAG = 8


def exact(left, right):
    return jnp.dot(left, right, precision=HIGHEST, preferred_element_type=jnp.float32)


def three_pass(left, right):
    high = left.astype(jnp.bfloat16)
    low = (left - high.astype(jnp.float32)).astype(jnp.bfloat16)

    def product(x, y):
        return jnp.dot(x, y, preferred_element_type=jnp.float32)

    return product(high, right[0]) + (product(low, right[0]) + product(high, right[1]))


def kernel(
    n_rows, n_cols, off_ref, f_hbm, m_hbm, fwd_hbm, inv_hbm, loc_hbm, eig_hbm, par_hbm,
    out_ref, rest_ref, f_ref, m_ref, fwd, inv, loc, eig_ref, par_ref,
    spill_out, spill_in, own, mine, theirs, ys, mom, sums, weigh, wave_f, wave_b,
    tab_sem, spill_send, spill_recv, x_send, x_recv, y_send, y_recv, m_send, m_recv, c_send, c_recv,
):
    a = lax.axis_index("rows")
    b = lax.axis_index("cols")
    n, w = out_ref.shape
    step = n // CHUNKS
    screen = 16.0 / (w * w)
    f32 = jnp.float32

    def load(k, src, dst):
        copy = pltpu.make_async_copy(src, dst, tab_sem.at[k])
        copy.start()
        return copy

    load_m = load(0, m_hbm, m_ref)
    load_f = load(1, f_hbm, f_ref)
    barrier = pltpu.get_barrier_semaphore()
    for k in range(1, n_rows):
        pl.semaphore_signal(barrier, inc=1, device_id={"rows": lax.rem(a + k, n_rows)}, device_id_type=MESH)
    for k in range(1, n_cols):
        pl.semaphore_signal(barrier, inc=1, device_id={"cols": lax.rem(b + k, n_cols)}, device_id_type=MESH)
    load_par = load(2, par_hbm, par_ref)
    load_fwd = load(3, fwd_hbm.at[b], fwd)
    load_loc = load(4, loc_hbm, loc)
    load_eig = load(5, eig_hbm, eig_ref)
    load_inv = load(6, inv_hbm.at[b], inv)

    s = off_ref[0, 0]

    def placing(first_row, count, first_t):
        r_at = lax.broadcasted_iota(jnp.int32, (count, n), 0) + first_row
        t_at = lax.broadcasted_iota(jnp.int32, (count, n), 1) + (first_t + s)
        return jnp.where(r_at == t_at, 1.0, 0.0).astype(jnp.bfloat16)

    def placed(matrix, pair):
        return jnp.dot(matrix, pair, preferred_element_type=f32)

    def pair_of(start):
        rows = pl.ds(start, n)
        return jnp.concatenate(
            [f_ref[rows, :], m_ref[rows, :].astype(f32).astype(jnp.bfloat16)], axis=1
        )

    first = placing(n - 2 * LAG, step + 2 * LAG, MARGIN)
    load_m.wait()
    load_f.wait()
    pair_low = pair_of(MARGIN)
    block = placed(first, pair_low)
    end_f, end_m = block[2 * LAG - 1 : 2 * LAG, :w], block[2 * LAG - 1 : 2 * LAG, w:]
    g_end = end_m * (block[2 * LAG : 2 * LAG + 1, :w] - end_f) / jnp.maximum(end_m, 1.0)
    spill_out[:LAG, :w] = jnp.broadcast_to(g_end, (LAG, w))
    spill_out[:LAG, w:] = jnp.zeros((LAG, w), f32)
    spill_out[LAG : LAG + step, :] = block[2 * LAG :]
    own[n : n + LAG, :] = block[2 * LAG : 3 * LAG]

    pl.semaphore_wait(barrier, n_rows - 1 + n_cols - 1)
    spill_copies = []
    for c in range(CHUNKS):
        lo = 0 if c == 0 else LAG + c * step
        rows = pl.ds(lo, LAG + (c + 1) * step - lo)
        if c > 0:
            spill_out[rows, :] = placed(placing(n + c * step, step, MARGIN), pair_low)
        spill_copies.append(
            pltpu.make_async_remote_copy(
                src_ref=spill_out.at[rows], dst_ref=spill_in.at[rows],
                send_sem=spill_send.at[c], recv_sem=spill_recv.at[c],
                device_id={"rows": lax.rem(a + 1, n_rows)}, device_id_type=MESH,
            )
        )
        pl.when(a < n_rows - 1)(spill_copies[-1].start)

    own[:n, :] = placed(placing(0, n, 0), pair_of(0))
    load_par.wait()
    row_f = lax.broadcasted_iota(jnp.int32, (n, w), 0).astype(f32)
    for c in range(n_cols):
        theta = par_ref[c, 0:1]
        wave_b[c] = jnp.exp(-theta * row_f)
        wave_f[c] = jnp.exp(-theta * ((n - 1) - row_f))
    mu = par_ref[b, 5:6]

    def all_waves(row):
        return jnp.concatenate([par_ref[c, row : row + 1] for c in range(n_cols)], axis=1)

    n_theta, wide_edge, tile_edge, tile_edge_q = [all_waves(row) for row in (1, 2, 3, 4)]
    period = 2 * n_rows

    def weight(power):
        return wide_edge * jnp.exp(-n_theta * power.astype(f32))

    for other in range(n_rows):
        weigh[0, other] = jnp.concatenate(
            [weight(lax.rem(a - 1 - other + period, period)), weight(a + other)], axis=1
        )
        weigh[1, other] = jnp.concatenate(
            [weight(period - 2 - a - other), weight(lax.rem(other - a - 1 + period, period))], axis=1
        )
    load_fwd.wait()
    spill_in[LAG + n :, :] = jnp.zeros((LAG, 2 * w), f32)

    @pl.when(a == 0)
    def _():
        spill_in[: LAG + n, :] = jnp.zeros((LAG + n, 2 * w), f32)

    def swap(source, target, send, recv, c):
        copies = []
        for k in range(1, n_cols):
            to = lax.rem(b + k, n_cols)
            copies.append(
                pltpu.make_async_remote_copy(
                    src_ref=source(to), dst_ref=target, send_sem=send.at[k, c], recv_sem=recv.at[k, c],
                    device_id={"cols": to}, device_id_type=MESH,
                )
            )
            copies[-1].start()
        return copies

    bounds = [0] + [c * step - LAG for c in range(1, CHUNKS)] + [n]
    mom_f = [jnp.zeros((1, w), f32)] * n_cols
    mom_b = [jnp.zeros((1, w), f32)] * n_cols
    gx_last = None
    swaps = []

    for c in range(CHUNKS):
        lo, hi = bounds[c], bounds[c + 1]
        count = hi - lo
        pl.when(a > 0)(spill_copies[c].wait_recv)
        row_at = lax.broadcasted_iota(jnp.int32, (count, w), 0)
        col_at = lax.broadcasted_iota(jnp.int32, (count, w), 1)
        last_col = col_at == w - 1
        f1, m1 = own[lo:hi, :w], own[lo:hi, w:]
        f2, m2 = spill_in[LAG + lo : LAG + hi, :w], spill_in[LAG + lo : LAG + hi, w:]
        down1 = own[lo + 1 : hi + 1, :w] - f1
        under = spill_in[LAG + lo + 1 : LAG + hi + 1, :]
        down2 = jnp.where(under[:, w:] > 0.0, under[:, :w] - f2, 0.0)
        across1 = jnp.where(last_col, 0.0, pltpu.roll(f1, w - 1, 1) - f1)
        across2 = jnp.where(last_col, 0.0, pltpu.roll(f2, w - 1, 1) - f2)
        scale = 1.0 / jnp.maximum(m1 + m2, 1.0)
        composite = (m1 * f1 + m2 * f2) * scale
        gx = (m1 * down1 + m2 * down2) * scale
        if c == CHUNKS - 1:
            gx = jnp.where((row_at == count - 1) & (a == n_rows - 1), 0.0, gx)
        gy = (m1 * across1 + m2 * across2) * scale
        before = spill_in[LAG - 1 : LAG, :w] if c == 0 else gx_last
        gx_before = jnp.where(row_at == 0, before, pltpu.roll(gx, 1, 0))
        gy_before = jnp.where(col_at == 0, 0.0, pltpu.roll(gy, 1, 1))
        gx_last = gx[count - 1 : count]
        right_side = screen * composite - ((gx - gx_before) + (gy - gy_before))
        for waves in range(n_cols):
            partial = exact(right_side, fwd[waves])
            mine[waves, lo:hi] = partial
            mom_f[waves] += jnp.sum(wave_f[waves, lo:hi] * partial, axis=0, keepdims=True)
            mom_b[waves] += jnp.sum(wave_b[waves, lo:hi] * partial, axis=0, keepdims=True)
        if c < CHUNKS - 1:
            rows = pl.ds(lo, count)
            swaps.append(swap(lambda to: mine.at[to, rows], theirs.at[b, rows], x_send, x_recv, c))

    sums[b] = jnp.concatenate(mom_f + mom_b, axis=1)
    sum_copies = swap(lambda to: sums.at[b], sums.at[b], c_send, c_recv, 0)
    rows = pl.ds(lo, count)
    swaps.append(swap(lambda to: mine.at[to, rows], theirs.at[b, rows], x_send, x_recv, CHUNKS - 1))
    for copy in sum_copies:
        copy.wait_recv()
    tile_sums = sums[0]
    for c in range(1, n_cols):
        tile_sums += sums[c]
    mom[a] = tile_sums
    m_copies = []
    for k in range(1, n_rows):
        m_copies.append(
            pltpu.make_async_remote_copy(
                src_ref=mom.at[a], dst_ref=mom.at[a], send_sem=m_send.at[k], recv_sem=m_recv.at[k],
                device_id={"rows": lax.rem(a + k, n_rows)}, device_id_type=MESH,
            )
        )
        m_copies[-1].start()
    load_loc.wait()
    load_eig.wait()
    for copies in swaps:
        for copy in copies:
            copy.wait_recv()
    spectral = mine[b]
    for k in range(1, n_cols):
        spectral += theirs[lax.rem(b + k, n_cols)]
    eig = jnp.concatenate([eig_ref[...]] * (w // 128), axis=1)
    quotient = exact(loc[0], spectral) / (eig + mu)
    ys[b] = exact(loc[1], quotient)
    y_copies = swap(lambda to: ys.at[b], ys.at[b], y_send, y_recv, 0)
    load_inv.wait()
    for copy in y_copies + m_copies:
        copy.wait_recv()
    top = jnp.zeros_like(tile_sums)
    bottom = jnp.zeros_like(tile_sums)
    for other in range(n_rows):
        top += weigh[0, other] * mom[other]
        bottom += weigh[1, other] * mom[other]
    width = n_cols * w
    own_f, own_b = tile_sums[:, :width], tile_sums[:, width:]
    from_top = top[:, :width] + top[:, width:] - (tile_edge * own_b + tile_edge_q * own_f)
    from_bottom = bottom[:, :width] + bottom[:, width:] - (tile_edge * own_f + tile_edge_q * own_b)

    def part(c):
        at = slice(c * w, (c + 1) * w)
        return three_pass(ys[c] + wave_b[c] * from_top[:, at] + wave_f[c] * from_bottom[:, at], inv[c])

    out_ref[...] = part(0)
    rest = jnp.zeros((n, w), f32)
    for c in range(1, n_cols):
        rest += part(c)
    rest_ref[...] = rest

    for copies in swaps + [sum_copies, y_copies, m_copies]:
        for copy in copies:
            copy.wait_send()
    for copy in spill_copies:
        pl.when(a < n_rows - 1)(copy.wait_send)


def shards(n_rows, n_cols, fields, masks, offsets):
    height, w = fields.shape
    n = height - MARGIN
    tables = make_tables(n, w, n_rows, n_cols)
    vmem = pl.BlockSpec(memory_space=pltpu.VMEM)
    anywhere = pl.BlockSpec(memory_space=pl.ANY)
    f32 = jnp.float32
    dma = pltpu.SemaphoreType.DMA
    out, rest = pl.pallas_call(
        functools.partial(kernel, n_rows, n_cols),
        out_shape=[jax.ShapeDtypeStruct((n, w), f32)] * 2,
        in_specs=[pl.BlockSpec(memory_space=pltpu.SMEM)] + [anywhere] * 7,
        out_specs=[vmem] * 2,
        scratch_shapes=[
            pltpu.VMEM((height, w), fields.dtype),
            pltpu.VMEM((height, w), masks.dtype),
            pltpu.VMEM((n_cols, w, w), f32),
            pltpu.VMEM((n_cols, 2, w, w), jnp.bfloat16),
            pltpu.VMEM((2, n, n), f32),
            pltpu.VMEM((n, 128), f32),
            pltpu.VMEM((n_cols, 8, w), f32),
            pltpu.VMEM((n + LAG, 2 * w), f32),
            pltpu.VMEM((n + 2 * LAG, 2 * w), f32),
            pltpu.VMEM((n + LAG, 2 * w), f32),
            pltpu.VMEM((n_cols, n, w), f32),
            pltpu.VMEM((n_cols, n, w), f32),
            pltpu.VMEM((n_cols, n, w), f32),
            pltpu.VMEM((n_rows, 1, 2 * n_cols * w), f32),
            pltpu.VMEM((n_cols, 1, 2 * n_cols * w), f32),
            pltpu.VMEM((2, n_rows, 1, 2 * n_cols * w), f32),
            pltpu.VMEM((n_cols, n, w), f32),
            pltpu.VMEM((n_cols, n, w), f32),
            dma((7,)),
            dma((CHUNKS,)),
            dma((CHUNKS,)),
            dma((n_cols, CHUNKS)),
            dma((n_cols, CHUNKS)),
            dma((n_cols, 1)),
            dma((n_cols, 1)),
            dma((n_rows,)),
            dma((n_rows,)),
            dma((n_cols, 1)),
            dma((n_cols, 1)),
        ],
        compiler_params=pltpu.CompilerParams(
            collective_id=0, has_side_effects=True, vmem_limit_bytes=40 * 1024 * 1024
        ),
    )(offsets, fields, masks, *tables)
    return out + rest


def solution(mesh):
    placed = (P("rows", "cols"), P("rows", "cols"), P("rows", "cols"))
    body = functools.partial(shards, mesh.shape["rows"], mesh.shape["cols"])
    return jax.shard_map(body, mesh=mesh, in_specs=placed, out_specs=P("rows", "cols"), check_vma=False)
```

```python
import functools
import math

import jax
import jax.numpy as jnp
import numpy as np
from jax import lax
from jax.experimental import pallas as pl
from jax.experimental.pallas import tpu as pltpu
from jax.sharding import PartitionSpec as P

MARGIN = 128
MESH = pl.DeviceIdType.MESH
HIGHEST = lax.Precision.HIGHEST


def cosine_matrix(length):
    k = np.arange(length)[:, None]
    i = np.arange(length)[None, :]
    table = np.cos(np.pi * (((2 * i + 1) * k) % (4 * length)) / (2 * length))
    table *= np.where(k == 0, math.sqrt(1.0 / length), math.sqrt(2.0 / length))
    return table


def make_tables(n, tile_cols, n_rows, n_cols):
    strip_cols = n_cols * tile_cols
    screen = 16.0 / (tile_cols * tile_cols)
    full = cosine_matrix(strip_cols)
    blocks = full.reshape(n_cols, tile_cols, n_cols, tile_cols)
    inverse = blocks.transpose(2, 0, 1, 3)
    forward = blocks.transpose(2, 0, 3, 1)
    inverse = inverse.astype(np.float32)
    high = inverse.astype(jnp.bfloat16)
    low = (inverse - high.astype(np.float32)).astype(jnp.bfloat16)
    inverse = np.stack([high, low], axis=2)
    local = cosine_matrix(n)
    row_eigen = 4.0 * np.sin(np.pi * np.arange(n) / (2 * n)) ** 2
    col_eigen = 4.0 * np.sin(np.pi * np.arange(strip_cols) / (2 * strip_cols)) ** 2
    mu = screen + col_eigen
    theta = 2.0 * np.arcsinh(np.sqrt(mu) / 2.0)
    edge = np.exp(-theta) / (2.0 * np.sinh(theta))
    q = np.exp(-n * theta)
    params = np.zeros((n_cols, 8, tile_cols))
    params[:, 0] = theta.reshape(n_cols, tile_cols)
    params[:, 1] = (n * theta).reshape(n_cols, tile_cols)
    params[:, 2] = (edge / (1.0 - q ** (2 * n_rows))).reshape(n_cols, tile_cols)
    params[:, 3] = (edge / (1.0 - q * q)).reshape(n_cols, tile_cols)
    params[:, 4] = (edge * q / (1.0 - q * q)).reshape(n_cols, tile_cols)
    params[:, 5] = mu.reshape(n_cols, tile_cols)
    eigen = np.broadcast_to(row_eigen[:, None], (n, 128))
    both = np.stack([local, local.T])
    forward, both, eigen, params = [
        np.ascontiguousarray(t, dtype=np.float32) for t in (forward, both, eigen, params)
    ]
    return forward, inverse, both, eigen, params


CHUNKS = 4
LAG = 8


def exact(left, right):
    return jnp.dot(left, right, precision=HIGHEST, preferred_element_type=jnp.float32)


def three_pass(left, right):
    high = left.astype(jnp.bfloat16)
    low = (left - high.astype(jnp.float32)).astype(jnp.bfloat16)

    def product(x, y):
        return jnp.dot(x, y, preferred_element_type=jnp.float32)

    return product(high, right[0]) + (product(low, right[0]) + product(high, right[1]))


def kernel(
    n_rows, n_cols, off_ref, f_hbm, m_hbm, fwd_hbm, inv_hbm, loc_hbm, eig_hbm, par_hbm,
    out_ref, rest_ref, f_ref, m_ref, fwd, inv, loc, eig_ref, par_ref,
    spill_out, spill_in, own, mine, theirs, ys, mom, sums, weigh, wave_f, wave_b,
    tab_sem, spill_send, spill_recv, x_send, x_recv, y_send, y_recv, m_send, m_recv, c_send, c_recv,
):
    a = lax.axis_index("rows")
    b = lax.axis_index("cols")
    n, w = out_ref.shape
    step = n // CHUNKS
    screen = 16.0 / (w * w)
    f32 = jnp.float32

    def load(k, src, dst):
        copy = pltpu.make_async_copy(src, dst, tab_sem.at[k])
        copy.start()
        return copy

    load_m = load(0, m_hbm, m_ref)
    load_f = load(1, f_hbm, f_ref)
    barrier = pltpu.get_barrier_semaphore()
    for k in range(1, n_rows):
        pl.semaphore_signal(barrier, inc=1, device_id={"rows": lax.rem(a + k, n_rows)}, device_id_type=MESH)
    for k in range(1, n_cols):
        pl.semaphore_signal(barrier, inc=1, device_id={"cols": lax.rem(b + k, n_cols)}, device_id_type=MESH)
    load_par = load(2, par_hbm, par_ref)
    load_fwd = load(3, fwd_hbm.at[b], fwd)
    load_loc = load(4, loc_hbm, loc)
    load_eig = load(5, eig_hbm, eig_ref)
    load_inv = load(6, inv_hbm.at[b], inv)

    s = off_ref[0, 0]

    def placing(first_row, count, first_t):
        r_at = lax.broadcasted_iota(jnp.int32, (count, n), 0) + first_row
        t_at = lax.broadcasted_iota(jnp.int32, (count, n), 1) + (first_t + s)
        return jnp.where(r_at == t_at, 1.0, 0.0).astype(jnp.bfloat16)

    def placed(matrix, pair):
        return jnp.dot(matrix, pair, preferred_element_type=f32)

    def pair_of(start):
        rows = pl.ds(start, n)
        return jnp.concatenate(
            [f_ref[rows, :], m_ref[rows, :].astype(f32).astype(jnp.bfloat16)], axis=1
        )

    first = placing(n - 2 * LAG, step + 2 * LAG, MARGIN)
    load_m.wait()
    load_f.wait()
    pair_low = pair_of(MARGIN)
    block = placed(first, pair_low)
    end_f, end_m = block[2 * LAG - 1 : 2 * LAG, :w], block[2 * LAG - 1 : 2 * LAG, w:]
    g_end = end_m * (block[2 * LAG : 2 * LAG + 1, :w] - end_f) / jnp.maximum(end_m, 1.0)
    spill_out[:LAG, :w] = jnp.broadcast_to(g_end, (LAG, w))
    spill_out[:LAG, w:] = jnp.zeros((LAG, w), f32)
    spill_out[LAG : LAG + step, :] = block[2 * LAG :]
    own[n : n + LAG, :] = block[2 * LAG : 3 * LAG]

    pl.semaphore_wait(barrier, n_rows - 1 + n_cols - 1)
    spill_copies = []
    for c in range(CHUNKS):
        lo = 0 if c == 0 else LAG + c * step
        rows = pl.ds(lo, LAG + (c + 1) * step - lo)
        if c > 0:
            spill_out[rows, :] = placed(placing(n + c * step, step, MARGIN), pair_low)
        spill_copies.append(
            pltpu.make_async_remote_copy(
                src_ref=spill_out.at[rows], dst_ref=spill_in.at[rows],
                send_sem=spill_send.at[c], recv_sem=spill_recv.at[c],
                device_id={"rows": lax.rem(a + 1, n_rows)}, device_id_type=MESH,
            )
        )
        pl.when(a < n_rows - 1)(spill_copies[-1].start)

    own[:n, :] = placed(placing(0, n, 0), pair_of(0))
    load_par.wait()
    row_f = lax.broadcasted_iota(jnp.int32, (n, w), 0).astype(f32)
    for c in range(n_cols):
        theta = par_ref[c, 0:1]
        wave_b[c] = jnp.exp(-theta * row_f)
        wave_f[c] = jnp.exp(-theta * ((n - 1) - row_f))
    mu = par_ref[b, 5:6]

    def all_waves(row):
        return jnp.concatenate([par_ref[c, row : row + 1] for c in range(n_cols)], axis=1)

    n_theta, wide_edge, tile_edge, tile_edge_q = [all_waves(row) for row in (1, 2, 3, 4)]
    period = 2 * n_rows

    def weight(power):
        return wide_edge * jnp.exp(-n_theta * power.astype(f32))

    for other in range(n_rows):
        weigh[0, other] = jnp.concatenate(
            [weight(lax.rem(a - 1 - other + period, period)), weight(a + other)], axis=1
        )
        weigh[1, other] = jnp.concatenate(
            [weight(period - 2 - a - other), weight(lax.rem(other - a - 1 + period, period))], axis=1
        )
    load_fwd.wait()
    spill_in[LAG + n :, :] = jnp.zeros((LAG, 2 * w), f32)

    @pl.when(a == 0)
    def _():
        spill_in[: LAG + n, :] = jnp.zeros((LAG + n, 2 * w), f32)

    def swap(source, target, send, recv, c):
        copies = []
        for k in range(1, n_cols):
            to = lax.rem(b + k, n_cols)
            copies.append(
                pltpu.make_async_remote_copy(
                    src_ref=source(to), dst_ref=target, send_sem=send.at[k, c], recv_sem=recv.at[k, c],
                    device_id={"cols": to}, device_id_type=MESH,
                )
            )
            copies[-1].start()
        return copies

    bounds = [0] + [c * step - LAG for c in range(1, CHUNKS)] + [n]
    mom_f = [jnp.zeros((1, w), f32)] * n_cols
    mom_b = [jnp.zeros((1, w), f32)] * n_cols
    gx_last = None
    swaps = []

    for c in range(CHUNKS):
        lo, hi = bounds[c], bounds[c + 1]
        count = hi - lo
        pl.when(a > 0)(spill_copies[c].wait_recv)
        row_at = lax.broadcasted_iota(jnp.int32, (count, w), 0)
        col_at = lax.broadcasted_iota(jnp.int32, (count, w), 1)
        last_col = col_at == w - 1
        f1, m1 = own[lo:hi, :w], own[lo:hi, w:]
        f2, m2 = spill_in[LAG + lo : LAG + hi, :w], spill_in[LAG + lo : LAG + hi, w:]
        down1 = own[lo + 1 : hi + 1, :w] - f1
        under = spill_in[LAG + lo + 1 : LAG + hi + 1, :]
        down2 = jnp.where(under[:, w:] > 0.0, under[:, :w] - f2, 0.0)
        across1 = jnp.where(last_col, 0.0, pltpu.roll(f1, w - 1, 1) - f1)
        across2 = jnp.where(last_col, 0.0, pltpu.roll(f2, w - 1, 1) - f2)
        scale = 1.0 / jnp.maximum(m1 + m2, 1.0)
        composite = (m1 * f1 + m2 * f2) * scale
        gx = (m1 * down1 + m2 * down2) * scale
        if c == CHUNKS - 1:
            gx = jnp.where((row_at == count - 1) & (a == n_rows - 1), 0.0, gx)
        gy = (m1 * across1 + m2 * across2) * scale
        before = spill_in[LAG - 1 : LAG, :w] if c == 0 else gx_last
        gx_before = jnp.where(row_at == 0, before, pltpu.roll(gx, 1, 0))
        gy_before = jnp.where(col_at == 0, 0.0, pltpu.roll(gy, 1, 1))
        gx_last = gx[count - 1 : count]
        right_side = screen * composite - ((gx - gx_before) + (gy - gy_before))
        for waves in range(n_cols):
            partial = exact(right_side, fwd[waves])
            mine[waves, lo:hi] = partial
            mom_f[waves] += jnp.sum(wave_f[waves, lo:hi] * partial, axis=0, keepdims=True)
            mom_b[waves] += jnp.sum(wave_b[waves, lo:hi] * partial, axis=0, keepdims=True)
        if c < CHUNKS - 1:
            rows = pl.ds(lo, count)
            swaps.append(swap(lambda to: mine.at[to, rows], theirs.at[b, rows], x_send, x_recv, c))

    sums[b] = jnp.concatenate(mom_f + mom_b, axis=1)
    sum_copies = swap(lambda to: sums.at[b], sums.at[b], c_send, c_recv, 0)
    rows = pl.ds(lo, count)
    swaps.append(swap(lambda to: mine.at[to, rows], theirs.at[b, rows], x_send, x_recv, CHUNKS - 1))
    for copy in sum_copies:
        copy.wait_recv()
    tile_sums = sums[0]
    for c in range(1, n_cols):
        tile_sums += sums[c]
    mom[a] = tile_sums
    m_copies = []
    for k in range(1, n_rows):
        m_copies.append(
            pltpu.make_async_remote_copy(
                src_ref=mom.at[a], dst_ref=mom.at[a], send_sem=m_send.at[k], recv_sem=m_recv.at[k],
                device_id={"rows": lax.rem(a + k, n_rows)}, device_id_type=MESH,
            )
        )
        m_copies[-1].start()
    load_loc.wait()
    load_eig.wait()
    for copies in swaps:
        for copy in copies:
            copy.wait_recv()
    spectral = mine[b]
    for k in range(1, n_cols):
        spectral += theirs[lax.rem(b + k, n_cols)]
    eig = jnp.concatenate([eig_ref[...]] * (w // 128), axis=1)
    quotient = exact(loc[0], spectral) / (eig + mu)
    ys[b] = exact(loc[1], quotient)
    y_copies = swap(lambda to: ys.at[b], ys.at[b], y_send, y_recv, 0)
    load_inv.wait()
    for copy in y_copies + m_copies:
        copy.wait_recv()
    top = jnp.zeros_like(tile_sums)
    bottom = jnp.zeros_like(tile_sums)
    for other in range(n_rows):
        top += weigh[0, other] * mom[other]
        bottom += weigh[1, other] * mom[other]
    width = n_cols * w
    own_f, own_b = tile_sums[:, :width], tile_sums[:, width:]
    from_top = top[:, :width] + top[:, width:] - (tile_edge * own_b + tile_edge_q * own_f)
    from_bottom = bottom[:, :width] + bottom[:, width:] - (tile_edge * own_f + tile_edge_q * own_b)

    def part(c):
        at = slice(c * w, (c + 1) * w)
        return three_pass(ys[c] + wave_b[c] * from_top[:, at] + wave_f[c] * from_bottom[:, at], inv[c])

    out_ref[...] = part(0)
    rest = jnp.zeros((n, w), f32)
    for c in range(1, n_cols):
        rest += part(c)
    rest_ref[...] = rest

    for copies in swaps + [sum_copies, y_copies, m_copies]:
        for copy in copies:
            copy.wait_send()
    for copy in spill_copies:
        pl.when(a < n_rows - 1)(copy.wait_send)


def shards(n_rows, n_cols, fields, masks, offsets):
    height, w = fields.shape
    n = height - MARGIN
    tables = make_tables(n, w, n_rows, n_cols)
    vmem = pl.BlockSpec(memory_space=pltpu.VMEM)
    anywhere = pl.BlockSpec(memory_space=pl.ANY)
    f32 = jnp.float32
    dma = pltpu.SemaphoreType.DMA
    out, rest = pl.pallas_call(
        functools.partial(kernel, n_rows, n_cols),
        out_shape=[jax.ShapeDtypeStruct((n, w), f32)] * 2,
        in_specs=[pl.BlockSpec(memory_space=pltpu.SMEM)] + [anywhere] * 7,
        out_specs=[vmem] * 2,
        scratch_shapes=[
            pltpu.VMEM((height, w), fields.dtype),
            pltpu.VMEM((height, w), masks.dtype),
            pltpu.VMEM((n_cols, w, w), f32),
            pltpu.VMEM((n_cols, 2, w, w), jnp.bfloat16),
            pltpu.VMEM((2, n, n), f32),
            pltpu.VMEM((n, 128), f32),
            pltpu.VMEM((n_cols, 8, w), f32),
            pltpu.VMEM((n + LAG, 2 * w), f32),
            pltpu.VMEM((n + 2 * LAG, 2 * w), f32),
            pltpu.VMEM((n + LAG, 2 * w), f32),
            pltpu.VMEM((n_cols, n, w), f32),
            pltpu.VMEM((n_cols, n, w), f32),
            pltpu.VMEM((n_cols, n, w), f32),
            pltpu.VMEM((n_rows, 1, 2 * n_cols * w), f32),
            pltpu.VMEM((n_cols, 1, 2 * n_cols * w), f32),
            pltpu.VMEM((2, n_rows, 1, 2 * n_cols * w), f32),
            pltpu.VMEM((n_cols, n, w), f32),
            pltpu.VMEM((n_cols, n, w), f32),
            dma((7,)),
            dma((CHUNKS,)),
            dma((CHUNKS,)),
            dma((n_cols, CHUNKS)),
            dma((n_cols, CHUNKS)),
            dma((n_cols, 1)),
            dma((n_cols, 1)),
            dma((n_rows,)),
            dma((n_rows,)),
            dma((n_cols, 1)),
            dma((n_cols, 1)),
        ],
        compiler_params=pltpu.CompilerParams(
            collective_id=0, has_side_effects=True, vmem_limit_bytes=56 * 1024 * 1024
        ),
    )(offsets, fields, masks, *tables)
    return out + rest


def solution(mesh):
    placed = (P("rows", "cols"), P("rows", "cols"), P("rows", "cols"))
    body = functools.partial(shards, mesh.shape["rows"], mesh.shape["cols"])
    return jax.shard_map(body, mesh=mesh, in_specs=placed, out_specs=P("rows", "cols"), check_vma=False)
```
